32 devices in a mesh: parts: 2 (over y), dp: 4 (over z), tensor: 4 (over x, core).
Axes of the slice: x: 2, y: 2, z: 4, core: 2. Of those that a mesh axis runs over, the one named last changes fastest.
Arguments:
- activations: bfloat16 [4096, 8192], P(('parts', 'dp', 'tensor')), parts along dimension 0, may hold values from -6 to 6
- query_cotangent: bfloat16 [4096, 8192], P(('parts', 'dp'), 'tensor'), parts along dimension 0, may hold values from -6 to 6
- value_cotangent: bfloat16 [4096, 1024], P(('parts', 'dp'), 'tensor'), parts along dimension 0, may hold values from -6 to 6
- query_matrix: bfloat16 [8192, 8192], P(None, 'tensor'), may hold values from -0.0625 to 0.0625
- value_matrix: bfloat16 [8192, 1024], P(None, 'tensor'), may hold values from -0.0625 to 0.0625
- block_tenant: int32 [64], P(('parts', 'dp')), parts along dimension 0, may hold values from 0 to 7
- owner_slot: int32 [16], P('parts'), parts along dimension 0, may hold values from 0 to 7, as said below
- slot_step: int32 [16], P(('parts', 'dp')), parts along dimension 0, may hold values from 1 to 2000
- down_state: float32 [16, 3, 2, 32, 8192], P(('parts', 'dp'), None, None, None, 'tensor'), parts along dimension 0, as said below
- query_state: float32 [16, 3, 32, 8192], P(('parts', 'dp'), None, None, 'tensor'), parts along dimension 0, as said below
- value_state: float32 [16, 3, 32, 1024], P(('parts', 'dp'), None, None, 'tensor'), parts along dimension 0, as said below
- serve_tenant: int32 [32], P('parts'), parts along dimension 0, may hold values from 0 to 7, as said below
Outputs:
- input_cotangent: bfloat16 [4096, 8192], P(('parts', 'dp', 'tensor')), parts along dimension 0
- new_down: float32 [16, 2, 2, 32, 8192], P(('parts', 'dp'), None, None, None, 'tensor'), parts along dimension 0
- new_down_master: float32 [16, 2, 32, 8192], P(('parts', 'dp'), None, None, 'tensor'), parts along dimension 0
- new_query: float32 [16, 3, 32, 8192], P(('parts', 'dp'), None, None, 'tensor'), parts along dimension 0
- new_value: float32 [16, 3, 32, 1024], P(('parts', 'dp'), None, None, 'tensor'), parts along dimension 0
- served_down: bfloat16 [32, 2, 32, 8192], P(('parts', 'dp'), None, None, 'tensor'), parts along dimension 0
- served_query: bfloat16 [32, 32, 8192], P(('parts', 'dp'), None, 'tensor'), parts along dimension 0
- served_value: bfloat16 [32, 32, 1024], P(('parts', 'dp'), None, 'tensor'), parts along dimension 0
The draws below stay inside these ranges and needn't reach their ends.
There are 2 independent parts, one for each index of `parts`. The reference program is written for one: setup_inputs(seed, part) draws one part's arguments, and reference() takes and returns one part's arrays. A program takes and returns all parts, laid end to end along the dimension named above; an argument that names none is the same for every part. Nothing has to cross between parts.
Inputs may be any that keep to these rules, and one draw needn't show every extreme that they name: `owner_slot`: each row number appears once; the tenants of rows s with equal s // 2 share an owner. `serve_tenant`: the 4 slots of one replica (slots 4 * r to 4 * r + 3) name tenants whose values owner_slot // 2 all differ. `down_state`: entry 2 along dimension 1 (second moments) lies in 0.1 to 10. `query_state`: entry 2 along dimension 1 (second moments) lies in 0.01 to 1. `value_state`: entry 2 along dimension 1 (second moments) lies in 0.01 to 1.
All inputs are finite; a program needn't handle non-finite values.
Results may differ from the reference program's by a relative error of at most 0.015.
Values may be sent and summed in bfloat16 or wider, within the bound.
A program may use at most 192 MiB of HBM per device.

```python
import math
import jax
import jax.numpy as jnp
import numpy as np
from jax import lax

MODEL_WIDTH = 8192
DV = 1024
R = 32
BLOCK = 64
TEN_OWN = 2
SERVE = 4
TENANTS = 8
TOTAL_TOKENS = 2048
BLOCKS = 32
REPLICAS = 4
N_TENSOR = 4


def slot_order(key):
    return jax.random.permutation(jax.random.fold_in(key, 11), TENANTS).astype(jnp.int32)


def state_normal(key, full_shape, scale_value, first_scale, low_log, high_log):
    subkeys = jax.random.split(key, 3)
    master = scale_value * jnp.clip(jax.random.normal(subkeys[0], full_shape, jnp.float32), -4.0, 4.0)
    first_moment = first_scale * jnp.clip(jax.random.normal(subkeys[1], full_shape, jnp.float32), -4.0, 4.0)
    second = jnp.exp(jax.random.uniform(subkeys[2], full_shape, jnp.float32, low_log, high_log))
    return jnp.stack([master, first_moment, second], axis=1)


def draw_owner_slot(key, part):
    return slot_order(key)


def draw_serve_tenant(key, part):
    slots = slot_order(key)
    key = jax.random.fold_in(key, 5)
    holder = jnp.argsort(slots, stable=True).astype(jnp.int32)
    subkeys = jax.random.split(key, REPLICAS)

    def one_replica(replica_key):
        owners = jax.random.permutation(jax.random.fold_in(replica_key, 1), REPLICAS)[:SERVE]
        pick_local = jax.random.randint(jax.random.fold_in(replica_key, 2), (SERVE,), 0, TEN_OWN)
        return holder[owners * TEN_OWN + pick_local]
    return jax.vmap(one_replica)(subkeys).reshape(-1).astype(jnp.int32)


def draw_down_state(key, part):
    key = jax.random.fold_in(key, 21)
    return state_normal(key, (TENANTS, 2, R, MODEL_WIDTH), MODEL_WIDTH ** (-0.5), 1.0, -2.3, 2.3)


def draw_query_state(key, part):
    key = jax.random.fold_in(key, 22)
    return state_normal(key, (TENANTS, R, MODEL_WIDTH), 8.0 * MODEL_WIDTH ** (-0.5), 0.2, -4.6, -0.001)


def draw_value_state(key, part):
    key = jax.random.fold_in(key, 23)
    return state_normal(key, (TENANTS, R, DV), 8.0 * DV ** (-0.5), 0.2, -4.6, -0.001)


def set_ends(result, stream_key, smallest, largest):
    extent = result.shape
    spot = [jax.random.randint(jax.random.fold_in(stream_key, axis), (), 0, extent[axis]) for axis in range(len(extent))]
    result = result.at[tuple(spot)].set(smallest)
    longest = extent.index(max(extent))
    spot[longest] = (spot[longest] + 1) % extent[longest]
    return result.at[tuple(spot)].set(largest)


def level_of(key, extent, cuts, smallest, largest):
    factor_of = 1.0
    for dim, parts in cuts:
        heights = jax.random.uniform(jax.random.fold_in(jax.random.fold_in(key, 6), dim), (parts,), jnp.float32, smallest / len(cuts), largest / len(cuts))
        factor_of = factor_of * jnp.repeat(jnp.exp(heights), extent[dim] // parts).reshape((-1,) + (1,) * (len(extent) - 1 - dim))
    return factor_of


def rank_table(amount, lean):
    loads = [(1 << 20) // math.isqrt(standing ** lean) + 1 for standing in range(1, amount + 1)]
    scale = 1 + sum(loads) // (1 << 30)
    return np.cumsum(np.array([max(1, weight // scale) for weight in loads]))


def ranked_ids(key, dims, amount, skew):
    grid = rank_table(amount, skew)
    pick = jax.random.randint(jax.random.fold_in(key, 1), dims, 0, int(grid[amount - 1]))
    grade = jnp.searchsorted(jnp.asarray(grid, jnp.int32), pick, side="right")
    return jax.random.permutation(jax.random.fold_in(key, 2), amount)[grade].astype(jnp.int32)


def scatter_about(rng, extent, scale, bound, pieces=(), held_as=jnp.bfloat16):
    array = scale * jax.random.normal(rng, extent, jnp.float32)
    if pieces:
        array = array * level_of(rng, extent, pieces, -0.22, 0.18)
    return jnp.clip(array, -bound, bound).astype(held_as)


def setup_inputs(seed: int = 0, part: int = 0) -> dict:
    key_list = jax.random.split(jax.random.key(seed), 13)
    part_keys = jax.random.split(jax.random.fold_in(key_list[12], part), 13)
    return {
        "activations": scatter_about(part_keys[0], (TOTAL_TOKENS, MODEL_WIDTH), 1.0, 6.0, ((0, 16),)),
        "query_cotangent": scatter_about(part_keys[1], (TOTAL_TOKENS, MODEL_WIDTH), 1.0, 6.0, ((0, 4), (1, 4))),
        "value_cotangent": scatter_about(part_keys[2], (TOTAL_TOKENS, DV), 1.0, 6.0, ((0, 4), (1, 4))),
        "query_matrix": scatter_about(key_list[3], (MODEL_WIDTH, MODEL_WIDTH), MODEL_WIDTH ** -0.5, 0.0625, ((1, 4),)),
        "value_matrix": scatter_about(key_list[4], (MODEL_WIDTH, DV), MODEL_WIDTH ** -0.5, 0.0625, ((1, 4),)),
        "block_tenant": set_ends(ranked_ids(part_keys[5], (BLOCKS,), TENANTS, 2), jax.random.fold_in(part_keys[5], 3), 0, TENANTS - 1).astype(jnp.int32),
        "owner_slot": draw_owner_slot(jax.random.fold_in(jax.random.fold_in(key_list[12], part), 71), part),
        "slot_step": set_ends(jax.random.randint(part_keys[7], (TENANTS,), 1, 2001), jax.random.fold_in(part_keys[7], 1), 1, 2000).astype(jnp.int32),
        "down_state": draw_down_state(jax.random.fold_in(jax.random.fold_in(key_list[12], part), 71), part),
        "query_state": draw_query_state(jax.random.fold_in(jax.random.fold_in(key_list[12], part), 71), part),
        "value_state": draw_value_state(jax.random.fold_in(jax.random.fold_in(key_list[12], part), 71), part),
        "serve_tenant": draw_serve_tenant(jax.random.fold_in(jax.random.fold_in(key_list[12], part), 71), part),
    }


ADAPTER_SCALE = 0.25
BETA_ONE = 0.9
BETA_TWO = 0.999
LEARN_RATE = 0.02
WEIGHT_DECAY = 0.01
ADAM_EPSILON = 1e-08

def adam_update(packed_state, gradient, counts):
    master = packed_state[:, 0]
    first_moment = BETA_ONE * packed_state[:, 1] + (1.0 - BETA_ONE) * gradient
    second = BETA_TWO * packed_state[:, 2] + (1.0 - BETA_TWO) * gradient * gradient
    shaped = counts.astype(jnp.float32).reshape((-1,) + (1,) * (gradient.ndim - 1))
    fix_one = 1.0 - jnp.exp(shaped * math.log(BETA_ONE))
    fix_two = 1.0 - jnp.exp(shaped * math.log(BETA_TWO))
    master = master - LEARN_RATE * (first_moment / fix_one / (jnp.sqrt(second / fix_two) + ADAM_EPSILON) + WEIGHT_DECAY * master)
    return jnp.stack([master, first_moment, second], axis=1)

def pieces_sum(query_cotangent, value_cotangent, query_matrix, value_matrix, adapter_output):
    column_width = MODEL_WIDTH // N_TENSOR
    value_width = DV // N_TENSOR

    def add_group(running, cluster_index):
        query_cols = lax.dynamic_slice_in_dim(query_cotangent, cluster_index * column_width, column_width, 1)
        query_weight = lax.dynamic_slice_in_dim(query_matrix, cluster_index * column_width, column_width, 1)
        value_cols = lax.dynamic_slice_in_dim(value_cotangent, cluster_index * value_width, value_width, 1)
        value_weight = lax.dynamic_slice_in_dim(value_matrix, cluster_index * value_width, value_width, 1)
        value_piece = jnp.dot(query_cols, query_weight.T, preferred_element_type=jnp.float32)
        value_piece = value_piece + jnp.dot(value_cols, value_weight.T, preferred_element_type=jnp.float32)
        column_start = lax.dynamic_slice_in_dim(value_piece, cluster_index * column_width, column_width, 1)
        adapter_columns = lax.dynamic_slice_in_dim(adapter_output, cluster_index * column_width, column_width, 1)
        value_piece = lax.dynamic_update_slice_in_dim(value_piece, column_start + adapter_columns, cluster_index * column_width, 1)
        value_piece = lax.optimization_barrier(value_piece.astype(jnp.bfloat16)).astype(jnp.float32)
        return (running + value_piece, None)
    running, _ = lax.scan(add_group, jnp.zeros((TOTAL_TOKENS, MODEL_WIDTH), jnp.float32), jnp.arange(N_TENSOR, dtype=jnp.int32))
    return running.astype(jnp.bfloat16)

def reference(activations, query_cotangent, value_cotangent, query_matrix, value_matrix, block_tenant, owner_slot, slot_step, down_state, query_state, value_state, serve_tenant):
    work_down = down_state[:, 0].astype(jnp.bfloat16)
    work_query = query_state[:, 0].astype(jnp.bfloat16)
    work_value = value_state[:, 0].astype(jnp.bfloat16)
    block_position = owner_slot[block_tenant].astype(jnp.int32)
    activation_blocks = activations.reshape(BLOCKS, BLOCK, MODEL_WIDTH)
    query_block_list = query_cotangent.reshape(BLOCKS, BLOCK, MODEL_WIDTH)
    value_block_list = value_cotangent.reshape(BLOCKS, BLOCK, DV)

    def block_width(block_items):
        act_block, query_row_set, value_row_set, slot_here = block_items
        reduce_block = work_down[slot_here].astype(jnp.float32)
        up_query = work_query[slot_here]
        up_value = work_value[slot_here]
        activation_full = act_block.astype(jnp.float32)
        narrow_hidden = jnp.einsum('bd,krd->bkr', activation_full, reduce_block).astype(jnp.bfloat16)
        back_query = jnp.dot(query_row_set, up_query.T, preferred_element_type=jnp.float32)
        back_value = jnp.dot(value_row_set, up_value.T, preferred_element_type=jnp.float32)
        low_u = jnp.stack([back_query, back_value], axis=1).astype(jnp.bfloat16)
        narrow_full = low_u.astype(jnp.float32)
        adapter_block = ADAPTER_SCALE * jnp.einsum('upj,pjh->uh', narrow_full, reduce_block)
        reduce_gradient_part = ADAPTER_SCALE * jnp.einsum('afy,ae->fye', narrow_full, activation_full)
        query_gradient_part = ADAPTER_SCALE * jnp.dot(narrow_hidden[:, 0].T, query_row_set, preferred_element_type=jnp.float32)
        value_gradient_part = ADAPTER_SCALE * jnp.dot(narrow_hidden[:, 1].T, value_row_set, preferred_element_type=jnp.float32)
        return (adapter_block, reduce_gradient_part, query_gradient_part, value_gradient_part)
    adapter_block_list, reduce_gradient_list, query_gradient_list, value_gradient_list = lax.map(block_width, (activation_blocks, query_block_list, value_block_list, block_position))
    adapter_output = adapter_block_list.reshape(TOTAL_TOKENS, MODEL_WIDTH)
    input_cotangent = pieces_sum(query_cotangent, value_cotangent, query_matrix, value_matrix, adapter_output)
    down_gradient = jax.ops.segment_sum(reduce_gradient_list, block_position, num_segments=TENANTS)
    query_gradient = jax.ops.segment_sum(query_gradient_list, block_position, num_segments=TENANTS)
    value_gradient = jax.ops.segment_sum(value_gradient_list, block_position, num_segments=TENANTS)
    down_full = adam_update(down_state, down_gradient, slot_step)
    new_down_master = down_full[:, 0]
    new_down = down_full[:, 1:]
    new_query = adam_update(query_state, query_gradient, slot_step)
    new_value = adam_update(value_state, value_gradient, slot_step)
    serve_rows = owner_slot[serve_tenant].astype(jnp.int32)
    served_down = new_down_master[serve_rows].astype(jnp.bfloat16)
    served_query = new_query[serve_rows, 0].astype(jnp.bfloat16)
    served_value = new_value[serve_rows, 0].astype(jnp.bfloat16)
    return (input_cotangent, new_down, new_down_master, new_query, new_value, served_down, served_query, served_value)
```

```python
import math

import jax
import jax.numpy as jnp
from jax import lax
from jax.sharding import PartitionSpec as P

ADAPTER_SCALE = 0.25
BETA_ONE = 0.9
BETA_TWO = 0.999
LEARN_RATE = 0.02
WEIGHT_DECAY = 0.01
ADAM_EPSILON = 1e-08

F32 = jnp.float32
BF16 = jnp.bfloat16


def dot(a, b, ca, cb):
    return lax.dot_general(a, b, (((ca,), (cb,)), ((), ())), preferred_element_type=F32)


def adam_parts(packed_state, gradient, counts):
    master = packed_state[:, 0]
    first = BETA_ONE * packed_state[:, 1] + (1.0 - BETA_ONE) * gradient
    second = BETA_TWO * packed_state[:, 2] + (1.0 - BETA_TWO) * gradient * gradient
    shaped = counts.astype(F32).reshape((-1,) + (1,) * (gradient.ndim - 1))
    fix_one = 1.0 - jnp.exp(shaped * math.log(BETA_ONE))
    fix_two = 1.0 - jnp.exp(shaped * math.log(BETA_TWO))
    master = master - LEARN_RATE * (
        first / fix_one / (jnp.sqrt(second / fix_two) + ADAM_EPSILON) + WEIGHT_DECAY * master
    )
    return master, first, second


def shifted(n, step):
    return [(i, (i + step) % n) for i in range(n)]


def line_gather(own, rank, n):
    right, left = [own], [own]
    for s in range(1, n):
        right.append(lax.ppermute(right[-1], "dp", [(i, i + 1) for i in range(s - 1, n - 1)]))
        left.append(lax.ppermute(left[-1], "dp", [(i, i - 1) for i in range(1, n - s + 1)]))
    return [own] + [jnp.where(rank >= s, right[s], left[n - s]) for s in range(1, n)]


def line_reduce(pieces, n):
    right = left = None
    for s in range(1, n):
        a, b = pieces[s], pieces[n - s]
        if right is not None:
            a, b = a + right.astype(F32), b + left.astype(F32)
        right = lax.ppermute(a.astype(BF16), "dp", [(i, i + 1) for i in range(0, s)])
        left = lax.ppermute(b.astype(BF16), "dp", [(i, i - 1) for i in range(n - s, n)])
    if right is None:
        return pieces[0]
    return pieces[0] + right.astype(F32) + left.astype(F32)


def body(
    activations,
    query_cotangent,
    value_cotangent,
    query_matrix,
    value_matrix,
    block_tenant,
    owner_slot,
    slot_step,
    down_state,
    query_state,
    value_state,
    serve_tenant,
):
    G = lax.axis_size("dp")
    T = lax.axis_size("tensor")
    g = lax.axis_index("dp")
    t = lax.axis_index("tensor")
    chips = T // 2
    core, chip = t % 2, t // 2
    tokens, width = query_cotangent.shape
    value_here = value_cotangent.shape[1]
    rows = activations.shape[0]
    features_all = query_matrix.shape[0]
    owned, rank = query_state.shape[0], query_state.shape[2]
    block_len = tokens // block_tenant.shape[0]
    served_here = serve_tenant.shape[0] // G

    own_query = query_state[:, 0].astype(BF16).reshape(owned * rank, width)
    own_value = value_state[:, 0].astype(BF16).reshape(owned * rank, value_here)
    own_down = down_state[:, 0].astype(BF16).reshape(owned * 2 * rank, width)
    query_pieces = line_gather(own_query, g, G)
    value_pieces = line_gather(own_value, g, G)
    down_pieces = line_gather(own_down, g, G)

    feats = jnp.zeros((T, rows, width), BF16)
    for s in range(T):
        part = lax.dynamic_slice_in_dim(activations, ((t + s) % T) * width, width, 1)
        if s:
            part = lax.ppermute(part, "tensor", shifted(T, s))
        feats = lax.dynamic_update_index_in_dim(feats, part, (t - s) % T, 0)
    feats = feats.reshape(tokens, width)

    position = jnp.repeat(owner_slot[block_tenant], block_len)
    masks = []
    for s in range(G):
        first_row = ((g - s) % G) * owned
        masks.append(
            (first_row + jnp.arange(owned, dtype=jnp.int32))[:, None] == position[None, :]
        )

    def pick(products):
        total = 0.0
        for s in range(G):
            p = products[s].reshape(owned, -1, tokens)
            total = total + jnp.sum(jnp.where(masks[s][:, None, :], p, 0.0), axis=0)
        return total

    def everywhere(part):
        part = part.astype(BF16)
        total = part.astype(F32)
        for s in range(1, T):
            total = total + lax.ppermute(part, "tensor", shifted(T, s)).astype(F32)
        return total.astype(BF16)

    def spread(low):
        return [
            jnp.where(m[:, None, :], low[None], jnp.zeros((), BF16)).reshape(-1, tokens)
            for m in masks
        ]

    back_q = pick([dot(w, query_cotangent, 1, 1) for w in query_pieces])
    back_v = pick([dot(w, value_cotangent, 1, 1) for w in value_pieces])
    low_u = everywhere(jnp.concatenate([back_q, back_v], axis=0))
    low_u_at = spread(low_u)

    def ordered(a):
        cut = [
            lax.dynamic_slice_in_dim(a, (2 * ((chip + k) % chips) + c) * rows, rows, 0)
            for c in (1 - core, core)
            for k in range(chips)
        ]
        return jnp.concatenate(cut, axis=0)

    lhs_q, lhs_v = ordered(query_cotangent), ordered(value_cotangent)
    half = chips * rows
    pieces = 4
    wide = features_all // pieces
    sibling = [(i, i ^ 1) for i in range(T)]
    frozen = []
    for j in range(pieces):
        cols = slice(j * wide, (j + 1) * wide)
        p = dot(lhs_q, query_matrix[cols], 1, 1) + dot(lhs_v, value_matrix[cols], 1, 1)
        p = p.astype(BF16)
        got = lax.ppermute(p[:half], "tensor", sibling)
        both = p[half:].astype(F32) + got.astype(F32)
        total = both[:rows]
        for k in range(1, chips):
            away = both[k * rows : (k + 1) * rows].astype(BF16)
            total = total + lax.ppermute(away, "tensor", shifted(T, 2 * k)).astype(F32)
        frozen.append(total)

    down_grad = line_reduce(
        [ADAPTER_SCALE * dot(u, feats, 1, 0) for u in low_u_at], G
    ).reshape(owned, 2, rank, width)

    low_h = everywhere(pick([dot(w, feats, 1, 1) for w in down_pieces]))
    query_grad = line_reduce(
        [ADAPTER_SCALE * dot(h, query_cotangent, 1, 0) for h in spread(low_h[:rank])], G
    ).reshape(owned, rank, width)
    value_grad = line_reduce(
        [ADAPTER_SCALE * dot(h, value_cotangent, 1, 0) for h in spread(low_h[rank:])], G
    ).reshape(owned, rank, value_here)

    lora = sum(dot(u, w, 0, 0) for u, w in zip(low_u_at, down_pieces))
    lora = (ADAPTER_SCALE * lora).astype(BF16)
    lora_parts = []
    for s in range(T):
        part = lax.dynamic_slice_in_dim(lora, ((t + s) % T) * rows, rows, 0)
        lora_parts.append(lax.ppermute(part, "tensor", shifted(T, s)) if s else part)
    lora_stack = jnp.stack(lora_parts)
    lora_cols = jnp.concatenate(
        [lax.dynamic_index_in_dim(lora_stack, (t - j) % T, 0, False) for j in range(T)], axis=1
    )
    input_cotangent = (jnp.concatenate(frozen, axis=1) + lora_cols.astype(F32)).astype(BF16)

    d_master, d_first, d_second = adam_parts(down_state, down_grad, slot_step)
    q_master, q_first, q_second = adam_parts(query_state, query_grad, slot_step)
    v_master, v_first, v_second = adam_parts(value_state, value_grad, slot_step)

    serve_rows = owner_slot[serve_tenant].reshape(G, served_here)

    def serve(master):
        fresh = master.astype(BF16)
        came = []
        for s in range(G):
            wanted = lax.dynamic_index_in_dim(serve_rows, (g + s) % G, 0, False)
            row = jnp.sum(jnp.where(wanted // owned == g, wanted % owned, 0))
            part = lax.dynamic_index_in_dim(fresh, row, 0, False)
            came.append(lax.ppermute(part, "dp", shifted(G, s)) if s else part)
        mine = lax.dynamic_index_in_dim(serve_rows, g, 0, False)
        distance = (g - mine // owned) % G
        out = []
        for q in range(served_here):
            piece = came[0]
            for s in range(1, G):
                piece = jnp.where(distance[q] == s, came[s], piece)
            out.append(piece)
        return jnp.stack(out)

    return (
        input_cotangent,
        jnp.stack([d_first, d_second], axis=1),
        d_master,
        jnp.stack([q_master, q_first, q_second], axis=1),
        jnp.stack([v_master, v_first, v_second], axis=1),
        serve(d_master),
        serve(q_master),
        serve(v_master),
    )


def solution(mesh):
    in_specs = (
        P(("parts", "dp", "tensor"), None),
        P(("parts", "dp"), "tensor"),
        P(("parts", "dp"), "tensor"),
        P(None, "tensor"),
        P(None, "tensor"),
        P(("parts", "dp")),
        P("parts"),
        P(("parts", "dp")),
        P(("parts", "dp"), None, None, None, "tensor"),
        P(("parts", "dp"), None, None, "tensor"),
        P(("parts", "dp"), None, None, "tensor"),
        P("parts"),
    )
    out_specs = (
        P(("parts", "dp", "tensor"), None),
        P(("parts", "dp"), None, None, None, "tensor"),
        P(("parts", "dp"), None, None, "tensor"),
        P(("parts", "dp"), None, None, "tensor"),
        P(("parts", "dp"), None, None, "tensor"),
        P(("parts", "dp"), None, None, "tensor"),
        P(("parts", "dp"), None, "tensor"),
        P(("parts", "dp"), None, "tensor"),
    )
    return jax.shard_map(body, mesh=mesh, in_specs=in_specs, out_specs=out_specs, check_vma=False)
```

```python
import functools
import math

import jax
import jax.numpy as jnp
from jax import lax
from jax.experimental import pallas as pl
from jax.experimental.pallas import tpu as pltpu
from jax.sharding import PartitionSpec as P

ADAPTER_SCALE = 0.25
BETA_ONE = 0.9
BETA_TWO = 0.999
LEARN_RATE = 0.02
WEIGHT_DECAY = 0.01
ADAM_EPSILON = 1e-08

F32 = jnp.float32
BF16 = jnp.bfloat16


def dot(a, b, ca, cb):
    return lax.dot_general(a, b, (((ca,), (cb,)), ((), ())), preferred_element_type=F32)


def adam_parts(packed_state, gradient, counts):
    master = packed_state[:, 0]
    first = BETA_ONE * packed_state[:, 1] + (1.0 - BETA_ONE) * gradient
    second = BETA_TWO * packed_state[:, 2] + (1.0 - BETA_TWO) * gradient * gradient
    shaped = counts.astype(F32).reshape((-1,) + (1,) * (gradient.ndim - 1))
    fix_one = 1.0 - jnp.exp(shaped * math.log(BETA_ONE))
    fix_two = 1.0 - jnp.exp(shaped * math.log(BETA_TWO))
    master = master - LEARN_RATE * (
        first / fix_one / (jnp.sqrt(second / fix_two) + ADAM_EPSILON) + WEIGHT_DECAY * master
    )
    return master, first, second


MESH = pl.DeviceIdType.MESH
ANY = pl.BlockSpec(memory_space=pl.ANY)
VMEM = pl.BlockSpec(memory_space=pltpu.VMEM)
DMA = pltpu.SemaphoreType.DMA


def meet(sizes):
    barrier = pltpu.get_barrier_semaphore()
    for axis, n in sizes.items():
        me = lax.axis_index(axis)
        for s in range(1, n):
            pl.semaphore_signal(
                barrier, inc=1, device_id={axis: lax.rem(me + s, n)}, device_id_type=MESH
            )
    pl.semaphore_wait(barrier, sum(n - 1 for n in sizes.values()))


def to_peer(axis, n, s, source, target, send, recv):
    me = lax.axis_index(axis)
    peer = lax.rem(me + s, n)
    return pltpu.make_async_remote_copy(
        src_ref=source(peer),
        dst_ref=target(me),
        send_sem=send.at[s],
        recv_sem=recv.at[s],
        device_id={axis: peer},
        device_id_type=MESH,
    )


def from_peer(axis, n, s, source, target, send, recv):
    me = lax.axis_index(axis)
    return pltpu.make_async_remote_copy(
        src_ref=source(lax.rem(me + s, n)),
        dst_ref=target(lax.rem(me + n - s, n)),
        send_sem=send.at[s],
        recv_sem=recv.at[s],
        device_id={axis: lax.rem(me + s, n)},
        device_id_type=MESH,
    )


def launch(jobs):
    for axis, n, source, target, send, recv in jobs:
        for s in range(1, n):
            to_peer(axis, n, s, source, target, send, recv).start()
    for axis, n, source, target, send, recv in jobs:
        me = lax.axis_index(axis)
        pltpu.make_async_copy(source(me), target(me), send.at[0]).start()


def finish(jobs):
    for axis, n, source, target, send, recv in jobs:
        me = lax.axis_index(axis)
        pltpu.make_async_copy(source(me), target(me), send.at[0]).wait()
        for s in range(1, n):
            to_peer(axis, n, s, source, target, send, recv).wait_send()
            from_peer(axis, n, s, source, target, send, recv).wait_recv()


def swap_kernel(sizes, axes, *refs):
    k = len(axes)
    sources, results, sems = refs[:k], refs[k : 2 * k], refs[2 * k :]
    meet(sizes)
    jobs = []
    for i, axis in enumerate(axes):
        source, result = sources[i], results[i]
        jobs.append(
            (
                axis,
                sizes[axis],
                lambda p, r=source: r.at[p],
                lambda p, r=result: r.at[p],
                sems[2 * i],
                sems[2 * i + 1],
            )
        )
    launch(jobs)
    finish(jobs)


def swap(arrays, axes, sizes, ident):
    sizes = {a: sizes[a] for a in sizes if a in axes}
    return pl.pallas_call(
        functools.partial(swap_kernel, sizes, axes),
        out_shape=[jax.ShapeDtypeStruct(a.shape, a.dtype) for a in arrays],
        in_specs=[ANY] * len(arrays),
        out_specs=[ANY] * len(arrays),
        scratch_shapes=[DMA((sizes[a],)) for a in axes for _ in range(2)],
        compiler_params=pltpu.CompilerParams(collective_id=ident, has_side_effects=True),
        name="swap_%d" % ident,
    )(*arrays)


def low_kernel(n, part, out, came, send, recv):
    meet({"tensor": n})
    for s in range(1, n):
        to_peer(
            "tensor", n, s, lambda p: part, lambda p: came.at[p], send, recv
        ).start()
    me = lax.axis_index("tensor")
    came[me] = part[...]
    for s in range(1, n):
        to_peer("tensor", n, s, lambda p: part, lambda p: came.at[p], send, recv).wait_send()
        from_peer("tensor", n, s, lambda p: part, lambda p: came.at[p], send, recv).wait_recv()
    total = came[0].astype(F32)
    for p in range(1, n):
        total = total + came[p].astype(F32)
    out[...] = total.astype(BF16)


def add_everywhere(part, n):
    return pl.pallas_call(
        functools.partial(low_kernel, n),
        out_shape=jax.ShapeDtypeStruct(part.shape, BF16),
        in_specs=[VMEM],
        out_specs=VMEM,
        scratch_shapes=[pltpu.VMEM((n,) + part.shape, BF16), DMA((n,)), DMA((n,))],
        compiler_params=pltpu.CompilerParams(collective_id=1, has_side_effects=True),
        name="low_sums",
    )(part)


def main_kernel(
    groups,
    n,
    lhs_q,
    lhs_v,
    query_matrix,
    value_matrix,
    activations,
    own_wide,
    own_value,
    out,
    feats,
    all_wide,
    all_value,
    weight,
    weight_v,
    part,
    near,
    mine,
    far,
    w_sem,
    wv_sem,
    near_send,
    near_recv,
    far_send,
    far_recv,
    feat_send,
    feat_recv,
    wide_send,
    wide_recv,
    value_send,
    value_recv,
):
    steps, cols = part.shape[0], part.shape[2]
    half = part.shape[1] // 2
    chips = n // 2
    rows = half // chips
    width = lhs_q.shape[1]
    t = lax.axis_index("tensor")
    chip, core = t // 2, lax.rem(t, 2)

    def load(j):
        slot = lax.rem(j, 2)
        at = pl.ds(pl.multiple_of(j * cols, cols), cols)
        return (
            pltpu.make_async_copy(query_matrix.at[at], weight.at[slot], w_sem.at[slot]),
            pltpu.make_async_copy(value_matrix.at[at], weight_v.at[slot], wv_sem.at[slot]),
        )

    for c in load(0):
        c.start()
    meet({"dp": groups, "tensor": n})
    jobs = [
        (
            "tensor",
            n,
            lambda p: activations.at[:, pl.ds(pl.multiple_of(p * width, width), width)],
            lambda p: feats.at[p],
            feat_send,
            feat_recv,
        ),
        ("dp", groups, lambda p: own_value, lambda p: all_value.at[p], value_send, value_recv),
        ("dp", groups, lambda p: own_wide, lambda p: all_wide.at[p], wide_send, wide_recv),
    ]
    launch(jobs)

    def near_copy(j):
        return pltpu.make_async_remote_copy(
            src_ref=part.at[j, pl.ds(0, half)],
            dst_ref=near.at[j],
            send_sem=near_send.at[j],
            recv_sem=near_recv.at[j],
            device_id={"tensor": 2 * chip + 1 - core},
            device_id_type=MESH,
        )

    def far_copy(k, j):
        return pltpu.make_async_remote_copy(
            src_ref=mine.at[k, j],
            dst_ref=far.at[k, j],
            send_sem=far_send.at[k, j],
            recv_sem=far_recv.at[k, j],
            device_id={"tensor": 2 * lax.rem(chip + k, chips) + core},
            device_id_type=MESH,
        )

    def join(j):
        near_copy(j).wait()
        for k in range(chips):
            here = pl.ds(half + k * rows, rows)
            there = pl.ds(k * rows, rows)
            both = part[j, here].astype(F32) + near[j, there].astype(F32)
            mine[k, j] = both.astype(BF16)
        for k in range(1, chips):
            far_copy(k, j).start()

    def step(j, carry):
        @pl.when(j + 1 < steps)
        def _():
            for c in load(j + 1):
                c.start()

        for c in load(j):
            c.wait()
        slot = lax.rem(j, 2)
        p = dot(lhs_q[...], weight[slot], 1, 1) + dot(lhs_v[...], weight_v[slot], 1, 1)
        part[j] = p.astype(BF16)
        near_copy(j).start()

        @pl.when(j >= 1)
        def _():
            join(j - 1)

        return carry

    lax.fori_loop(0, steps, step, 0)
    join(steps - 1)

    def last(j, carry):
        total = mine[0, j].astype(F32)
        for k in range(1, chips):
            far_copy(k, j).wait()
            total = total + far[k, j].astype(F32)
        out[j] = total.astype(BF16)
        return carry

    lax.fori_loop(0, steps, last, 0)
    finish(jobs)


def main_call(groups, n, lhs_q, lhs_v, query_matrix, value_matrix, activations, own_wide, own_value):
    tokens, width = lhs_q.shape
    rows = activations.shape[0]
    cols = 512
    steps = query_matrix.shape[0] // cols
    chips = n // 2
    half = tokens // 2
    s = jax.ShapeDtypeStruct
    return pl.pallas_call(
        functools.partial(main_kernel, groups, n),
        out_shape=[
            s((steps, rows, cols), BF16),
            s((n, rows, width), BF16),
            s((groups,) + own_wide.shape, BF16),
            s((groups,) + own_value.shape, BF16),
        ],
        in_specs=[VMEM, VMEM] + [ANY] * 5,
        out_specs=[VMEM, ANY, ANY, ANY],
        scratch_shapes=[
            pltpu.VMEM((2, cols, width), BF16),
            pltpu.VMEM((2, cols, lhs_v.shape[1]), BF16),
            pltpu.VMEM((steps, tokens, cols), BF16),
            pltpu.VMEM((steps, half, cols), BF16),
            pltpu.VMEM((chips, steps, rows, cols), BF16),
            pltpu.VMEM((chips, steps, rows, cols), BF16),
            DMA((2,)),
            DMA((2,)),
            DMA((steps,)),
            DMA((steps,)),
            DMA((chips, steps)),
            DMA((chips, steps)),
            DMA((n,)),
            DMA((n,)),
            DMA((groups,)),
            DMA((groups,)),
            DMA((groups,)),
            DMA((groups,)),
        ],
        compiler_params=pltpu.CompilerParams(
            collective_id=0, has_side_effects=True, vmem_limit_bytes=48 * 1024 * 1024
        ),
        name="frozen_and_gathers",
    )(lhs_q, lhs_v, query_matrix, value_matrix, activations, own_wide, own_value)


def body(
    activations,
    query_cotangent,
    value_cotangent,
    query_matrix,
    value_matrix,
    block_tenant,
    owner_slot,
    slot_step,
    down_state,
    query_state,
    value_state,
    serve_tenant,
):
    G = lax.axis_size("dp")
    T = lax.axis_size("tensor")
    sizes = {"dp": G, "tensor": T}
    g = lax.axis_index("dp")
    t = lax.axis_index("tensor")
    chips = T // 2
    core, chip = t % 2, t // 2
    tokens, width = query_cotangent.shape
    value_here = value_cotangent.shape[1]
    rows = activations.shape[0]
    owned, rank = query_state.shape[0], query_state.shape[2]
    slots = owned * G
    block_len = tokens // block_tenant.shape[0]
    served_here = serve_tenant.shape[0] // G

    own_wide = jnp.concatenate(
        [query_state[:, 0].reshape(owned * rank, width), down_state[:, 0].reshape(-1, width)], axis=0
    ).astype(BF16)
    own_value = value_state[:, 0].astype(BF16).reshape(owned * rank, value_here)

    def ordered(a):
        cut = [
            lax.dynamic_slice_in_dim(a, (2 * ((chip + k) % chips) + c) * rows, rows, 0)
            for c in (1 - core, core)
            for k in range(chips)
        ]
        return jnp.concatenate(cut, axis=0)

    frozen, feats, all_wide, all_value = main_call(
        G,
        T,
        ordered(query_cotangent),
        ordered(value_cotangent),
        query_matrix,
        value_matrix,
        activations,
        own_wide,
        own_value,
    )
    feats = feats.reshape(tokens, width)
    work_query = all_wide[:, : owned * rank].reshape(slots * rank, width)
    work_down = all_wide[:, owned * rank :].reshape(slots * 2 * rank, width)
    work_value = all_value.reshape(slots * rank, value_here)

    position = jnp.repeat(owner_slot[block_tenant], block_len)
    mask = jnp.arange(slots, dtype=jnp.int32)[:, None, None] == position[None, None, :]

    def pick(product):
        p = product.reshape(slots, -1, tokens)
        return jnp.sum(jnp.where(mask, p, 0.0), axis=0)

    def spread(low):
        return jnp.where(mask, low[None], jnp.zeros((), BF16)).reshape(-1, tokens)

    part = jnp.concatenate(
        [
            pick(dot(work_query, query_cotangent, 1, 1)),
            pick(dot(work_value, value_cotangent, 1, 1)),
            pick(dot(work_down, feats, 1, 1)),
        ],
        axis=0,
    ).astype(BF16)
    low = add_everywhere(part, T)
    low_u, low_h = low[: 2 * rank], low[2 * rank :]
    low_u_at = spread(low_u)

    down_part = (ADAPTER_SCALE * dot(low_u_at, feats, 1, 0)).astype(BF16)
    query_part = (ADAPTER_SCALE * dot(spread(low_h[:rank]), query_cotangent, 1, 0)).astype(BF16)
    value_part = (ADAPTER_SCALE * dot(spread(low_h[rank:]), value_cotangent, 1, 0)).astype(BF16)
    lora = (ADAPTER_SCALE * dot(low_u_at, work_down, 0, 0)).astype(BF16)

    down_came, query_came, value_came, lora_came = swap(
        [
            down_part.reshape(G, owned * 2 * rank, width),
            query_part.reshape(G, owned * rank, width),
            value_part.reshape(G, owned * rank, value_here),
            lora.reshape(T, rows, width),
        ],
        ("dp", "dp", "dp", "tensor"),
        sizes,
        2,
    )
    down_grad = jnp.sum(down_came.astype(F32), axis=0).reshape(owned, 2, rank, width)
    query_grad = jnp.sum(query_came.astype(F32), axis=0).reshape(owned, rank, width)
    value_grad = jnp.sum(value_came.astype(F32), axis=0).reshape(owned, rank, value_here)

    d_master, d_first, d_second = adam_parts(down_state, down_grad, slot_step)
    q_master, q_first, q_second = adam_parts(query_state, query_grad, slot_step)
    v_master, v_first, v_second = adam_parts(value_state, value_grad, slot_step)

    serve_rows = owner_slot[serve_tenant].reshape(G, served_here)
    row = jnp.sum(jnp.where(serve_rows // owned == g, serve_rows % owned, 0), axis=1)

    def wanted(master):
        fresh = master.astype(BF16)[None]
        pick_row = row.reshape((-1,) + (1,) * (fresh.ndim - 2))
        out = fresh[:, 0]
        for r in range(1, owned):
            out = jnp.where(pick_row == r, fresh[:, r], out)
        return out

    down_new, query_new, value_new = swap(
        [wanted(d_master), wanted(q_master), wanted(v_master)], ("dp",) * 3, sizes, 3
    )
    owner = lax.dynamic_index_in_dim(serve_rows, g, 0, False) // owned

    def served(came):
        return jnp.stack(
            [lax.dynamic_index_in_dim(came, owner[q], 0, False) for q in range(served_here)]
        )

    lora_cols = jnp.swapaxes(lora_came, 0, 1).reshape(rows, T * width)
    base = jnp.swapaxes(frozen, 0, 1).reshape(rows, T * width)
    input_cotangent = (base.astype(F32) + lora_cols.astype(F32)).astype(BF16)

    return (
        input_cotangent,
        jnp.stack([d_first, d_second], axis=1),
        d_master,
        jnp.stack([q_master, q_first, q_second], axis=1),
        jnp.stack([v_master, v_first, v_second], axis=1),
        served(down_new),
        served(query_new),
        served(value_new),
    )


def solution(mesh):
    in_specs = (
        P(("parts", "dp", "tensor"), None),
        P(("parts", "dp"), "tensor"),
        P(("parts", "dp"), "tensor"),
        P(None, "tensor"),
        P(None, "tensor"),
        P(("parts", "dp")),
        P("parts"),
        P(("parts", "dp")),
        P(("parts", "dp"), None, None, None, "tensor"),
        P(("parts", "dp"), None, None, "tensor"),
        P(("parts", "dp"), None, None, "tensor"),
        P("parts"),
    )
    out_specs = (
        P(("parts", "dp", "tensor"), None),
        P(("parts", "dp"), None, None, None, "tensor"),
        P(("parts", "dp"), None, None, "tensor"),
        P(("parts", "dp"), None, None, "tensor"),
        P(("parts", "dp"), None, None, "tensor"),
        P(("parts", "dp"), None, None, "tensor"),
        P(("parts", "dp"), None, "tensor"),
        P(("parts", "dp"), None, "tensor"),
    )
    return jax.shard_map(body, mesh=mesh, in_specs=in_specs, out_specs=out_specs, check_vma=False)
```

```python
import functools
import math

import jax
import jax.numpy as jnp
from jax import lax
from jax.experimental import pallas as pl
from jax.experimental.pallas import tpu as pltpu
from jax.sharding import PartitionSpec as P

ADAPTER_SCALE = 0.25
BETA_ONE = 0.9
BETA_TWO = 0.999
LEARN_RATE = 0.02
WEIGHT_DECAY = 0.01
ADAM_EPSILON = 1e-08

F32 = jnp.float32
BF16 = jnp.bfloat16


def dot(a, b, ca, cb):
    return lax.dot_general(a, b, (((ca,), (cb,)), ((), ())), preferred_element_type=F32)


MESH = pl.DeviceIdType.MESH
ANY = pl.BlockSpec(memory_space=pl.ANY)
VMEM = pl.BlockSpec(memory_space=pltpu.VMEM)
DMA = pltpu.SemaphoreType.DMA


def meet(sizes):
    barrier = pltpu.get_barrier_semaphore()
    for axis, n in sizes.items():
        me = lax.axis_index(axis)
        for s in range(1, n):
            pl.semaphore_signal(
                barrier, inc=1, device_id={axis: lax.rem(me + s, n)}, device_id_type=MESH
            )
    pl.semaphore_wait(barrier, sum(n - 1 for n in sizes.values()))


def to_peer(axis, n, s, source, target, send, recv):
    me = lax.axis_index(axis)
    peer = lax.rem(me + s, n)
    return pltpu.make_async_remote_copy(
        src_ref=source(peer),
        dst_ref=target(me),
        send_sem=send.at[s],
        recv_sem=recv.at[s],
        device_id={axis: peer},
        device_id_type=MESH,
    )


def from_peer(axis, n, s, source, target, send, recv):
    me = lax.axis_index(axis)
    return pltpu.make_async_remote_copy(
        src_ref=source(lax.rem(me + s, n)),
        dst_ref=target(lax.rem(me + n - s, n)),
        send_sem=send.at[s],
        recv_sem=recv.at[s],
        device_id={axis: lax.rem(me + s, n)},
        device_id_type=MESH,
    )


def launch(jobs):
    for axis, n, source, target, send, recv in jobs:
        for s in range(1, n):
            to_peer(axis, n, s, source, target, send, recv).start()
    for axis, n, source, target, send, recv in jobs:
        me = lax.axis_index(axis)
        pltpu.make_async_copy(source(me), target(me), send.at[0]).start()


def finish(jobs):
    for axis, n, source, target, send, recv in jobs:
        me = lax.axis_index(axis)
        pltpu.make_async_copy(source(me), target(me), send.at[0]).wait()
        for s in range(1, n):
            to_peer(axis, n, s, source, target, send, recv).wait_send()
            from_peer(axis, n, s, source, target, send, recv).wait_recv()


def swap_kernel(sizes, axes, *refs):
    k = len(axes)
    sources, results, sems = refs[:k], refs[k : 2 * k], refs[2 * k :]
    meet(sizes)
    jobs = []
    for i, axis in enumerate(axes):
        source, result = sources[i], results[i]
        jobs.append(
            (
                axis,
                sizes[axis],
                lambda p, r=source: r.at[p],
                lambda p, r=result: r.at[p],
                sems[2 * i],
                sems[2 * i + 1],
            )
        )
    launch(jobs)
    finish(jobs)


def swap(arrays, axes, sizes, ident):
    sizes = {a: sizes[a] for a in sizes if a in axes}
    return pl.pallas_call(
        functools.partial(swap_kernel, sizes, axes),
        out_shape=[jax.ShapeDtypeStruct(a.shape, a.dtype) for a in arrays],
        in_specs=[ANY] * len(arrays),
        out_specs=[ANY] * len(arrays),
        scratch_shapes=[DMA((sizes[a],)) for a in axes for _ in range(2)],
        compiler_params=pltpu.CompilerParams(collective_id=ident, has_side_effects=True),
        name="swap_%d" % ident,
    )(*arrays)


def line_kernel(sizes, chunks, k, *refs):
    parts, lora, sums, lora_came = refs[:k], refs[k], refs[k + 1 : 2 * k + 1], refs[2 * k + 1]
    scratch = refs[2 * k + 2 :]
    lora_send, lora_recv = scratch[:2]
    m = len(chunks)
    out_bufs, in_bufs = scratch[2 : 2 + m], scratch[2 + m : 2 + 2 * m]
    sends, recvs = scratch[2 + 2 * m : 2 + 3 * m], scratch[2 + 3 * m : 2 + 4 * m]
    n = sizes["dp"]
    g = lax.axis_index("dp")
    meet(sizes)
    jobs = [
        (
            "tensor",
            sizes["tensor"],
            lambda p: lora.at[p],
            lambda p: lora_came.at[:, pl.ds(pl.multiple_of(p * lora.shape[2], lora.shape[2]), lora.shape[2])],
            lora_send,
            lora_recv,
        )
    ]
    launch(jobs)

    def hop(c, way, s):
        ahead = lax.rem(g + 1, n) if way == 0 else lax.rem(g + n - 1, n)
        return pltpu.make_async_remote_copy(
            src_ref=out_bufs[c].at[way, s],
            dst_ref=in_bufs[c].at[way, s],
            send_sem=sends[c].at[way, s],
            recv_sem=recvs[c].at[way, s],
            device_id={"dp": ahead},
            device_id_type=MESH,
        )

    place = (g, n - 1 - g)
    for s in range(1, n):
        for way in (0, 1):

            @pl.when(place[way] < s)
            def _():
                goal = g + (n - s) if way == 0 else g - (n - s)
                for c, (i, lo, rows) in enumerate(chunks):
                    term = parts[i][goal, lo : lo + rows]

                    @pl.when(place[way] == 0)
                    def _():
                        out_bufs[c][way, s] = term

                    if s > 1:

                        @pl.when(place[way] > 0)
                        def _():
                            hop(c, way, s - 1).wait_recv()
                            out_bufs[c][way, s] = (
                                term.astype(F32) + in_bufs[c][way, s - 1].astype(F32)
                            ).astype(BF16)

                    hop(c, way, s).start()

    for c, (i, lo, rows) in enumerate(chunks):
        sums[i][lo : lo + rows] = parts[i][g, lo : lo + rows].astype(F32)
        for way in (0, 1):

            @pl.when(place[way] > 0)
            def _():
                hop(c, way, n - 1).wait_recv()
                sums[i][lo : lo + rows] = sums[i][lo : lo + rows] + in_bufs[c][way, n - 1].astype(F32)

    for s in range(1, n):
        for way in (0, 1):

            @pl.when(place[way] < s)
            def _():
                for c in range(m):
                    hop(c, way, s).wait_send()

    finish(jobs)


def line_sums(parts, lora, sizes, rows):
    k = len(parts)
    chunks = [(i, lo, rows) for i, a in enumerate(parts) for lo in range(0, a.shape[1], rows)]
    bufs = [pltpu.VMEM((2, sizes["dp"], r, parts[i].shape[2]), BF16) for i, _, r in chunks]
    sems = [DMA((2, sizes["dp"])) for _ in chunks]
    n = sizes["tensor"]
    return pl.pallas_call(
        functools.partial(line_kernel, sizes, chunks, k),
        out_shape=[jax.ShapeDtypeStruct(a.shape[1:], F32) for a in parts]
        + [jax.ShapeDtypeStruct((lora.shape[1], lora.shape[0] * lora.shape[2]), BF16)],
        in_specs=[VMEM] * k + [ANY],
        out_specs=[VMEM] * k + [ANY],
        scratch_shapes=[DMA((n,)), DMA((n,))] + bufs + bufs + sems + sems,
        compiler_params=pltpu.CompilerParams(
            collective_id=2, has_side_effects=True, vmem_limit_bytes=48 * 1024 * 1024
        ),
        name="line_sums",
    )(*parts, lora)


def adam_kernel(split, fix, row, state, grad, *outs):
    owned = state.shape[0]
    fresh = []
    for s in range(owned):
        gradient = grad[s]
        master = state[s, 0]
        first = BETA_ONE * state[s, 1] + (1.0 - BETA_ONE) * gradient
        second = BETA_TWO * state[s, 2] + (1.0 - BETA_TWO) * gradient * gradient
        master = master - LEARN_RATE * (
            first / fix[0, s] / (jnp.sqrt(second / fix[1, s]) + ADAM_EPSILON)
            + WEIGHT_DECAY * master
        )
        if split:
            outs[0][s] = master
            outs[1][s, 0] = first
            outs[1][s, 1] = second
        else:
            outs[0][s, 0] = master
            outs[0][s, 1] = first
            outs[0][s, 2] = second
        fresh.append(master.astype(BF16))
    for r in range(outs[-1].shape[0]):
        outs[-1][r] = fresh[0]
        for s in range(1, owned):

            @pl.when(row[r] == s)
            def _():
                outs[-1][r] = fresh[s]


def adam(state, grad, fix, row, split):
    owned, _, rows, width = state.shape
    cols = min(512, width)
    kinds = [((owned, rows, width), F32), ((owned, 2, rows, width), F32)]
    if not split:
        kinds = [((owned, 3, rows, width), F32)]
    kinds.append(((row.shape[0], rows, width), BF16))

    def spec(shape):
        lead = len(shape) - 1
        return pl.BlockSpec(tuple(shape[:-1]) + (cols,), lambda j: (0,) * lead + (j,))

    smem = pl.BlockSpec(memory_space=pltpu.SMEM)
    return pl.pallas_call(
        functools.partial(adam_kernel, split),
        grid=(width // cols,),
        out_shape=[jax.ShapeDtypeStruct(a, d) for a, d in kinds],
        in_specs=[smem, smem, spec(state.shape), spec(grad.shape)],
        out_specs=[spec(a) for a, _ in kinds],
        compiler_params=pltpu.CompilerParams(vmem_limit_bytes=48 * 1024 * 1024),
        name="adam",
    )(fix, row, state, grad)


def low_kernel(n, part, out, came, send, recv):
    meet({"tensor": n})
    for s in range(1, n):
        to_peer(
            "tensor", n, s, lambda p: part, lambda p: came.at[p], send, recv
        ).start()
    me = lax.axis_index("tensor")
    came[me] = part[...]
    for s in range(1, n):
        to_peer("tensor", n, s, lambda p: part, lambda p: came.at[p], send, recv).wait_send()
        from_peer("tensor", n, s, lambda p: part, lambda p: came.at[p], send, recv).wait_recv()
    total = came[0].astype(F32)
    for p in range(1, n):
        total = total + came[p].astype(F32)
    out[...] = total.astype(BF16)


def add_everywhere(part, n):
    return pl.pallas_call(
        functools.partial(low_kernel, n),
        out_shape=jax.ShapeDtypeStruct(part.shape, BF16),
        in_specs=[VMEM],
        out_specs=VMEM,
        scratch_shapes=[pltpu.VMEM((n,) + part.shape, BF16), DMA((n,)), DMA((n,))],
        compiler_params=pltpu.CompilerParams(collective_id=1, has_side_effects=True),
        name="low_sums",
    )(part)


def main_kernel(
    groups,
    n,
    lhs_q,
    lhs_v,
    query_matrix,
    value_matrix,
    activations,
    own_wide,
    own_value,
    out,
    feats,
    all_wide,
    all_value,
    weight,
    weight_v,
    part,
    near,
    mine,
    far,
    w_sem,
    wv_sem,
    near_send,
    near_recv,
    far_send,
    far_recv,
    feat_send,
    feat_recv,
    wide_send,
    wide_recv,
    value_send,
    value_recv,
):
    steps, cols = part.shape[0], part.shape[2]
    half = part.shape[1] // 2
    chips = n // 2
    rows = half // chips
    width = lhs_q.shape[1]
    t = lax.axis_index("tensor")
    chip, core = t // 2, lax.rem(t, 2)

    def load(j):
        slot = lax.rem(j, 2)
        at = pl.ds(pl.multiple_of(j * cols, cols), cols)
        return (
            pltpu.make_async_copy(query_matrix.at[at], weight.at[slot], w_sem.at[slot]),
            pltpu.make_async_copy(value_matrix.at[at], weight_v.at[slot], wv_sem.at[slot]),
        )

    for c in load(0):
        c.start()
    meet({"dp": groups, "tensor": n})
    jobs = [
        (
            "tensor",
            n,
            lambda p: activations.at[:, pl.ds(pl.multiple_of(p * width, width), width)],
            lambda p: feats.at[p],
            feat_send,
            feat_recv,
        ),
        ("dp", groups, lambda p: own_value, lambda p: all_value.at[p], value_send, value_recv),
        ("dp", groups, lambda p: own_wide, lambda p: all_wide.at[p], wide_send, wide_recv),
    ]
    launch(jobs)

    def near_copy(j):
        return pltpu.make_async_remote_copy(
            src_ref=part.at[j, pl.ds(0, half)],
            dst_ref=near.at[j],
            send_sem=near_send.at[j],
            recv_sem=near_recv.at[j],
            device_id={"tensor": 2 * chip + 1 - core},
            device_id_type=MESH,
        )

    def far_copy(k, j):
        return pltpu.make_async_remote_copy(
            src_ref=mine.at[k, j],
            dst_ref=far.at[k, j],
            send_sem=far_send.at[k, j],
            recv_sem=far_recv.at[k, j],
            device_id={"tensor": 2 * lax.rem(chip + k, chips) + core},
            device_id_type=MESH,
        )

    def join(j):
        near_copy(j).wait()
        for k in range(chips):
            here = pl.ds(half + k * rows, rows)
            there = pl.ds(k * rows, rows)
            both = part[j, here].astype(F32) + near[j, there].astype(F32)
            mine[k, j] = both.astype(BF16)
        for k in range(1, chips):
            far_copy(k, j).start()

    def step(j, carry):
        @pl.when(j + 1 < steps)
        def _():
            for c in load(j + 1):
                c.start()

        for c in load(j):
            c.wait()
        slot = lax.rem(j, 2)
        p = dot(lhs_q[...], weight[slot], 1, 1) + dot(lhs_v[...], weight_v[slot], 1, 1)
        part[j] = p.astype(BF16)
        near_copy(j).start()

        @pl.when(j >= 1)
        def _():
            join(j - 1)

        return carry

    lax.fori_loop(0, steps, step, 0)
    join(steps - 1)

    def last(j, carry):
        total = mine[0, j].astype(F32)
        for k in range(1, chips):
            far_copy(k, j).wait()
            total = total + far[k, j].astype(F32)
        out[:, pl.ds(pl.multiple_of(j * cols, cols), cols)] = total.astype(BF16)
        return carry

    lax.fori_loop(0, steps, last, 0)
    finish(jobs)


def main_call(groups, n, lhs_q, lhs_v, query_matrix, value_matrix, activations, own_wide, own_value):
    tokens, width = lhs_q.shape
    rows = activations.shape[0]
    cols = 512
    steps = query_matrix.shape[0] // cols
    chips = n // 2
    half = tokens // 2
    s = jax.ShapeDtypeStruct
    return pl.pallas_call(
        functools.partial(main_kernel, groups, n),
        out_shape=[
            s((rows, steps * cols), BF16),
            s((n, rows, width), BF16),
            s((groups,) + own_wide.shape, BF16),
            s((groups,) + own_value.shape, BF16),
        ],
        in_specs=[VMEM, VMEM] + [ANY] * 5,
        out_specs=[VMEM, ANY, ANY, ANY],
        scratch_shapes=[
            pltpu.VMEM((2, cols, width), BF16),
            pltpu.VMEM((2, cols, lhs_v.shape[1]), BF16),
            pltpu.VMEM((steps, tokens, cols), BF16),
            pltpu.VMEM((steps, half, cols), BF16),
            pltpu.VMEM((chips, steps, rows, cols), BF16),
            pltpu.VMEM((chips, steps, rows, cols), BF16),
            DMA((2,)),
            DMA((2,)),
            DMA((steps,)),
            DMA((steps,)),
            DMA((chips, steps)),
            DMA((chips, steps)),
            DMA((n,)),
            DMA((n,)),
            DMA((groups,)),
            DMA((groups,)),
            DMA((groups,)),
            DMA((groups,)),
        ],
        compiler_params=pltpu.CompilerParams(
            collective_id=0, has_side_effects=True, vmem_limit_bytes=48 * 1024 * 1024
        ),
        name="frozen_and_gathers",
    )(lhs_q, lhs_v, query_matrix, value_matrix, activations, own_wide, own_value)


def body(
    activations,
    query_cotangent,
    value_cotangent,
    query_matrix,
    value_matrix,
    block_tenant,
    owner_slot,
    slot_step,
    down_state,
    query_state,
    value_state,
    serve_tenant,
):
    G = lax.axis_size("dp")
    T = lax.axis_size("tensor")
    sizes = {"dp": G, "tensor": T}
    g = lax.axis_index("dp")
    t = lax.axis_index("tensor")
    chips = T // 2
    core, chip = t % 2, t // 2
    tokens, width = query_cotangent.shape
    value_here = value_cotangent.shape[1]
    rows = activations.shape[0]
    owned, rank = query_state.shape[0], query_state.shape[2]
    slots = owned * G
    block_len = tokens // block_tenant.shape[0]
    served_here = serve_tenant.shape[0] // G

    own_wide = jnp.concatenate(
        [query_state[:, 0].reshape(owned * rank, width), down_state[:, 0].reshape(-1, width)], axis=0
    ).astype(BF16)
    own_value = value_state[:, 0].astype(BF16).reshape(owned * rank, value_here)

    def ordered(a):
        cut = [
            lax.dynamic_slice_in_dim(a, (2 * ((chip + k) % chips) + c) * rows, rows, 0)
            for c in (1 - core, core)
            for k in range(chips)
        ]
        return jnp.concatenate(cut, axis=0)

    frozen, feats, all_wide, all_value = main_call(
        G,
        T,
        ordered(query_cotangent),
        ordered(value_cotangent),
        query_matrix,
        value_matrix,
        activations,
        own_wide,
        own_value,
    )
    feats = feats.reshape(tokens, width)
    work_query = all_wide[:, : owned * rank].reshape(slots * rank, width)
    work_down = all_wide[:, owned * rank :].reshape(slots * 2 * rank, width)
    work_value = all_value.reshape(slots * rank, value_here)

    position = jnp.repeat(owner_slot[block_tenant], block_len)
    mask = jnp.arange(slots, dtype=jnp.int32)[:, None, None] == position[None, None, :]

    def pick(product):
        p = product.reshape(slots, -1, tokens)
        return jnp.sum(jnp.where(mask, p, 0.0), axis=0)

    def spread(low):
        return jnp.where(mask, low[None], jnp.zeros((), BF16)).reshape(-1, tokens)

    part = jnp.concatenate(
        [
            pick(dot(work_query, query_cotangent, 1, 1)),
            pick(dot(work_value, value_cotangent, 1, 1)),
            pick(dot(work_down, feats, 1, 1)),
        ],
        axis=0,
    ).astype(BF16)
    low = add_everywhere(part, T)
    low_u, low_h = low[: 2 * rank], low[2 * rank :]
    low_u_at = spread(low_u)

    down_part = (ADAPTER_SCALE * dot(low_u_at, feats, 1, 0)).astype(BF16)
    query_part = (ADAPTER_SCALE * dot(spread(low_h[:rank]), query_cotangent, 1, 0)).astype(BF16)
    value_part = (ADAPTER_SCALE * dot(spread(low_h[rank:]), value_cotangent, 1, 0)).astype(BF16)
    lora = (ADAPTER_SCALE * dot(low_u_at, work_down, 0, 0)).astype(BF16)

    down_grad, query_grad, value_grad, lora_came = line_sums(
        [
            down_part.reshape(G, owned * 2 * rank, width),
            query_part.reshape(G, owned * rank, width),
            value_part.reshape(G, owned * rank, value_here),
        ],
        lora.reshape(T, rows, width),
        sizes,
        owned * rank,
    )

    serve_rows = owner_slot[serve_tenant].reshape(G, served_here)
    row = jnp.sum(jnp.where(serve_rows // owned == g, serve_rows % owned, 0), axis=1)
    counts = slot_step.astype(F32)
    fix = jnp.stack(
        [1.0 - jnp.exp(counts * math.log(BETA_ONE)), 1.0 - jnp.exp(counts * math.log(BETA_TWO))]
    )
    d_master, d_moments, d_wanted = adam(
        down_state.reshape(owned, 3, 2 * rank, width),
        down_grad.reshape(owned, 2 * rank, width),
        fix,
        row,
        True,
    )
    new_query, q_wanted = adam(
        query_state, query_grad.reshape(owned, rank, width), fix, row, False
    )
    new_value, v_wanted = adam(
        value_state, value_grad.reshape(owned, rank, value_here), fix, row, False
    )
    down_new, query_new, value_new = swap(
        [d_wanted, q_wanted, v_wanted], ("dp",) * 3, sizes, 3
    )
    owner = lax.dynamic_index_in_dim(serve_rows, g, 0, False) // owned

    def served(came):
        return jnp.stack(
            [lax.dynamic_index_in_dim(came, owner[q], 0, False) for q in range(served_here)]
        )

    input_cotangent = (frozen.astype(F32) + lora_came.astype(F32)).astype(BF16)

    return (
        input_cotangent,
        d_moments.reshape(owned, 2, 2, rank, width),
        d_master.reshape(owned, 2, rank, width),
        new_query,
        new_value,
        served(down_new).reshape(served_here, 2, rank, width),
        served(query_new),
        served(value_new),
    )


def solution(mesh):
    in_specs = (
        P(("parts", "dp", "tensor"), None),
        P(("parts", "dp"), "tensor"),
        P(("parts", "dp"), "tensor"),
        P(None, "tensor"),
        P(None, "tensor"),
        P(("parts", "dp")),
        P("parts"),
        P(("parts", "dp")),
        P(("parts", "dp"), None, None, None, "tensor"),
        P(("parts", "dp"), None, None, "tensor"),
        P(("parts", "dp"), None, None, "tensor"),
        P("parts"),
    )
    out_specs = (
        P(("parts", "dp", "tensor"), None),
        P(("parts", "dp"), None, None, None, "tensor"),
        P(("parts", "dp"), None, None, "tensor"),
        P(("parts", "dp"), None, None, "tensor"),
        P(("parts", "dp"), None, None, "tensor"),
        P(("parts", "dp"), None, None, "tensor"),
        P(("parts", "dp"), None, "tensor"),
        P(("parts", "dp"), None, "tensor"),
    )
    return jax.shard_map(body, mesh=mesh, in_specs=in_specs, out_specs=out_specs, check_vma=False)
```

```python
import functools
import math

import jax
import jax.numpy as jnp
from jax import lax
from jax.experimental import pallas as pl
from jax.experimental.pallas import tpu as pltpu
from jax.sharding import PartitionSpec as P

ADAPTER_SCALE = 0.25
BETA_ONE = 0.9
BETA_TWO = 0.999
LEARN_RATE = 0.02
WEIGHT_DECAY = 0.01
ADAM_EPSILON = 1e-08

F32 = jnp.float32
BF16 = jnp.bfloat16


def dot(a, b, ca, cb):
    return lax.dot_general(a, b, (((ca,), (cb,)), ((), ())), preferred_element_type=F32)


MESH = pl.DeviceIdType.MESH
ANY = pl.BlockSpec(memory_space=pl.ANY)
VMEM = pl.BlockSpec(memory_space=pltpu.VMEM)
DMA = pltpu.SemaphoreType.DMA


def meet(sizes):
    barrier = pltpu.get_barrier_semaphore()
    for axis, n in sizes.items():
        me = lax.axis_index(axis)
        for s in range(1, n):
            pl.semaphore_signal(
                barrier, inc=1, device_id={axis: lax.rem(me + s, n)}, device_id_type=MESH
            )
    pl.semaphore_wait(barrier, sum(n - 1 for n in sizes.values()))


def to_peer(axis, n, s, source, target, send, recv):
    me = lax.axis_index(axis)
    peer = lax.rem(me + s, n)
    return pltpu.make_async_remote_copy(
        src_ref=source(peer),
        dst_ref=target(me),
        send_sem=send.at[s],
        recv_sem=recv.at[s],
        device_id={axis: peer},
        device_id_type=MESH,
    )


def from_peer(axis, n, s, source, target, send, recv):
    me = lax.axis_index(axis)
    return pltpu.make_async_remote_copy(
        src_ref=source(lax.rem(me + s, n)),
        dst_ref=target(lax.rem(me + n - s, n)),
        send_sem=send.at[s],
        recv_sem=recv.at[s],
        device_id={axis: lax.rem(me + s, n)},
        device_id_type=MESH,
    )


def launch(jobs):
    for axis, n, source, target, send, recv in jobs:
        for s in range(1, n):
            to_peer(axis, n, s, source, target, send, recv).start()
    for axis, n, source, target, send, recv in jobs:
        me = lax.axis_index(axis)
        pltpu.make_async_copy(source(me), target(me), send.at[0]).start()


def finish(jobs):
    for axis, n, source, target, send, recv in jobs:
        me = lax.axis_index(axis)
        pltpu.make_async_copy(source(me), target(me), send.at[0]).wait()
        for s in range(1, n):
            to_peer(axis, n, s, source, target, send, recv).wait_send()
            from_peer(axis, n, s, source, target, send, recv).wait_recv()


def swap_kernel(sizes, axes, *refs):
    k = len(axes)
    sources, results, sems = refs[:k], refs[k : 2 * k], refs[2 * k :]
    meet(sizes)
    jobs = []
    for i, axis in enumerate(axes):
        source, result = sources[i], results[i]
        jobs.append(
            (
                axis,
                sizes[axis],
                lambda p, r=source: r.at[p],
                lambda p, r=result: r.at[p],
                sems[2 * i],
                sems[2 * i + 1],
            )
        )
    launch(jobs)
    finish(jobs)


def swap(arrays, axes, sizes, ident):
    sizes = {a: sizes[a] for a in sizes if a in axes}
    return pl.pallas_call(
        functools.partial(swap_kernel, sizes, axes),
        out_shape=[jax.ShapeDtypeStruct(a.shape, a.dtype) for a in arrays],
        in_specs=[ANY] * len(arrays),
        out_specs=[ANY] * len(arrays),
        scratch_shapes=[DMA((sizes[a],)) for a in axes for _ in range(2)],
        compiler_params=pltpu.CompilerParams(collective_id=ident, has_side_effects=True),
        name="swap_%d" % ident,
    )(*arrays)


def line_kernel(sizes, chunks, k, *refs):
    parts, lora, sums, lora_came = refs[:k], refs[k], refs[k + 1 : 2 * k + 1], refs[2 * k + 1]
    scratch = refs[2 * k + 2 :]
    lora_send, lora_recv = scratch[:2]
    m = len(chunks)
    out_bufs, in_bufs = scratch[2 : 2 + m], scratch[2 + m : 2 + 2 * m]
    sends, recvs = scratch[2 + 2 * m : 2 + 3 * m], scratch[2 + 3 * m : 2 + 4 * m]
    n = sizes["dp"]
    g = lax.axis_index("dp")
    meet(sizes)
    jobs = [
        (
            "tensor",
            sizes["tensor"],
            lambda p: lora.at[p],
            lambda p: lora_came.at[:, pl.ds(pl.multiple_of(p * lora.shape[2], lora.shape[2]), lora.shape[2])],
            lora_send,
            lora_recv,
        )
    ]
    launch(jobs)

    def hop(c, way, s):
        ahead = lax.rem(g + 1, n) if way == 0 else lax.rem(g + n - 1, n)
        return pltpu.make_async_remote_copy(
            src_ref=out_bufs[c].at[way, s],
            dst_ref=in_bufs[c].at[way, s],
            send_sem=sends[c].at[way, s],
            recv_sem=recvs[c].at[way, s],
            device_id={"dp": ahead},
            device_id_type=MESH,
        )

    place = (g, n - 1 - g)
    for s in range(1, n):
        for way in (0, 1):

            @pl.when(place[way] < s)
            def _():
                goal = g + (n - s) if way == 0 else g - (n - s)
                for c, (i, lo, rows) in enumerate(chunks):
                    term = parts[i][goal, lo : lo + rows]

                    @pl.when(place[way] == 0)
                    def _():
                        out_bufs[c][way, s] = term

                    if s > 1:

                        @pl.when(place[way] > 0)
                        def _():
                            hop(c, way, s - 1).wait_recv()
                            out_bufs[c][way, s] = (
                                term.astype(F32) + in_bufs[c][way, s - 1].astype(F32)
                            ).astype(BF16)

                    hop(c, way, s).start()

    for c, (i, lo, rows) in enumerate(chunks):
        sums[i][lo : lo + rows] = parts[i][g, lo : lo + rows].astype(F32)
        for way in (0, 1):

            @pl.when(place[way] > 0)
            def _():
                hop(c, way, n - 1).wait_recv()
                sums[i][lo : lo + rows] = sums[i][lo : lo + rows] + in_bufs[c][way, n - 1].astype(F32)

    for s in range(1, n):
        for way in (0, 1):

            @pl.when(place[way] < s)
            def _():
                for c in range(m):
                    hop(c, way, s).wait_send()

    finish(jobs)


def line_sums(parts, lora, sizes, rows):
    k = len(parts)
    chunks = [(i, lo, rows) for i, a in enumerate(parts) for lo in range(0, a.shape[1], rows)]
    bufs = [pltpu.VMEM((2, sizes["dp"], r, parts[i].shape[2]), BF16) for i, _, r in chunks]
    sems = [DMA((2, sizes["dp"])) for _ in chunks]
    n = sizes["tensor"]
    return pl.pallas_call(
        functools.partial(line_kernel, sizes, chunks, k),
        out_shape=[jax.ShapeDtypeStruct(a.shape[1:], F32) for a in parts]
        + [jax.ShapeDtypeStruct((lora.shape[1], lora.shape[0] * lora.shape[2]), BF16)],
        in_specs=[VMEM] * k + [ANY],
        out_specs=[VMEM] * k + [ANY],
        scratch_shapes=[DMA((n,)), DMA((n,))] + bufs + bufs + sems + sems,
        compiler_params=pltpu.CompilerParams(
            collective_id=2, has_side_effects=True, vmem_limit_bytes=48 * 1024 * 1024
        ),
        name="line_sums",
    )(*parts, lora)


def adam_kernel(split, fix, row, state, grad, *outs):
    owned = state.shape[0]
    fresh = []
    for s in range(owned):
        gradient = grad[s]
        master = state[s, 0]
        first = BETA_ONE * state[s, 1] + (1.0 - BETA_ONE) * gradient
        second = BETA_TWO * state[s, 2] + (1.0 - BETA_TWO) * gradient * gradient
        master = master - LEARN_RATE * (
            first / fix[0, s] / (jnp.sqrt(second / fix[1, s]) + ADAM_EPSILON)
            + WEIGHT_DECAY * master
        )
        if split:
            outs[0][s] = master
            outs[1][s, 0] = first
            outs[1][s, 1] = second
        else:
            outs[0][s, 0] = master
            outs[0][s, 1] = first
            outs[0][s, 2] = second
        fresh.append(master.astype(BF16))
    for r in range(outs[-1].shape[0]):
        outs[-1][r] = fresh[0]
        for s in range(1, owned):

            @pl.when(row[r] == s)
            def _():
                outs[-1][r] = fresh[s]


def adam(state, grad, fix, row, split):
    owned, _, rows, width = state.shape
    cols = min(512, width)
    kinds = [((owned, rows, width), F32), ((owned, 2, rows, width), F32)]
    if not split:
        kinds = [((owned, 3, rows, width), F32)]
    kinds.append(((row.shape[0], rows, width), BF16))

    def spec(shape):
        lead = len(shape) - 1
        return pl.BlockSpec(tuple(shape[:-1]) + (cols,), lambda j: (0,) * lead + (j,))

    smem = pl.BlockSpec(memory_space=pltpu.SMEM)
    return pl.pallas_call(
        functools.partial(adam_kernel, split),
        grid=(width // cols,),
        out_shape=[jax.ShapeDtypeStruct(a, d) for a, d in kinds],
        in_specs=[smem, smem, spec(state.shape), spec(grad.shape)],
        out_specs=[spec(a) for a, _ in kinds],
        compiler_params=pltpu.CompilerParams(vmem_limit_bytes=48 * 1024 * 1024),
        name="adam",
    )(fix, row, state, grad)


def slots_kernel(owner, *refs):
    k = len(refs) // 2
    for came, out in zip(refs[:k], refs[k:]):
        for q in range(out.shape[0]):
            for p in range(came.shape[0]):

                @pl.when(owner[q] == p)
                def _():
                    out[q] = came[p]


def served(owner, arrays):
    k = len(arrays)
    return pl.pallas_call(
        slots_kernel,
        out_shape=[
            jax.ShapeDtypeStruct(owner.shape + a.shape[1:], a.dtype) for a in arrays
        ],
        in_specs=[pl.BlockSpec(memory_space=pltpu.SMEM)] + [VMEM] * k,
        out_specs=[VMEM] * k,
        compiler_params=pltpu.CompilerParams(vmem_limit_bytes=48 * 1024 * 1024),
        name="serving_slots",
    )(owner, *arrays)


def low_kernel(n, part, out, came, send, recv):
    meet({"tensor": n})
    for s in range(1, n):
        to_peer(
            "tensor", n, s, lambda p: part, lambda p: came.at[p], send, recv
        ).start()
    me = lax.axis_index("tensor")
    came[me] = part[...]
    for s in range(1, n):
        to_peer("tensor", n, s, lambda p: part, lambda p: came.at[p], send, recv).wait_send()
        from_peer("tensor", n, s, lambda p: part, lambda p: came.at[p], send, recv).wait_recv()
    total = came[0].astype(F32)
    for p in range(1, n):
        total = total + came[p].astype(F32)
    out[...] = total.astype(BF16)


def add_everywhere(part, n):
    return pl.pallas_call(
        functools.partial(low_kernel, n),
        out_shape=jax.ShapeDtypeStruct(part.shape, BF16),
        in_specs=[VMEM],
        out_specs=VMEM,
        scratch_shapes=[pltpu.VMEM((n,) + part.shape, BF16), DMA((n,)), DMA((n,))],
        compiler_params=pltpu.CompilerParams(collective_id=1, has_side_effects=True),
        name="low_sums",
    )(part)


def main_kernel(
    groups,
    n,
    lhs_q,
    lhs_v,
    query_matrix,
    value_matrix,
    activations,
    own_query,
    own_down,
    own_value,
    out,
    feats,
    all_query,
    all_down,
    all_value,
    weight,
    weight_v,
    part,
    near,
    mine,
    far,
    w_sem,
    wv_sem,
    near_send,
    near_recv,
    far_send,
    far_recv,
    feat_send,
    feat_recv,
    query_send,
    query_recv,
    down_send,
    down_recv,
    value_send,
    value_recv,
):
    steps, cols = part.shape[0], part.shape[2]
    half = part.shape[1] // 2
    chips = n // 2
    rows = half // chips
    width = lhs_q.shape[1]
    t = lax.axis_index("tensor")
    chip, core = t // 2, lax.rem(t, 2)

    def load(j):
        slot = lax.rem(j, 2)
        at = pl.ds(pl.multiple_of(j * cols, cols), cols)
        return (
            pltpu.make_async_copy(query_matrix.at[at], weight.at[slot], w_sem.at[slot]),
            pltpu.make_async_copy(value_matrix.at[at], weight_v.at[slot], wv_sem.at[slot]),
        )

    for c in load(0):
        c.start()
    meet({"dp": groups, "tensor": n})
    jobs = [
        (
            "tensor",
            n,
            lambda p: activations.at[:, pl.ds(pl.multiple_of(p * width, width), width)],
            lambda p: feats.at[p],
            feat_send,
            feat_recv,
        ),
        ("dp", groups, lambda p: own_value, lambda p: all_value.at[p], value_send, value_recv),
        ("dp", groups, lambda p: own_query, lambda p: all_query.at[p], query_send, query_recv),
        ("dp", groups, lambda p: own_down, lambda p: all_down.at[p], down_send, down_recv),
    ]
    launch(jobs)

    def near_copy(j):
        return pltpu.make_async_remote_copy(
            src_ref=part.at[j, pl.ds(0, half)],
            dst_ref=near.at[j],
            send_sem=near_send.at[j],
            recv_sem=near_recv.at[j],
            device_id={"tensor": 2 * chip + 1 - core},
            device_id_type=MESH,
        )

    def far_copy(k, j):
        return pltpu.make_async_remote_copy(
            src_ref=mine.at[k, j],
            dst_ref=far.at[k, j],
            send_sem=far_send.at[k, j],
            recv_sem=far_recv.at[k, j],
            device_id={"tensor": 2 * lax.rem(chip + k, chips) + core},
            device_id_type=MESH,
        )

    def join(j):
        near_copy(j).wait()
        for k in range(chips):
            here = pl.ds(half + k * rows, rows)
            there = pl.ds(k * rows, rows)
            both = part[j, here].astype(F32) + near[j, there].astype(F32)
            mine[k, j] = both.astype(BF16)
        for k in range(1, chips):
            far_copy(k, j).start()

    def step(j, carry):
        @pl.when(j + 1 < steps)
        def _():
            for c in load(j + 1):
                c.start()

        for c in load(j):
            c.wait()
        slot = lax.rem(j, 2)
        p = dot(lhs_q[...], weight[slot], 1, 1) + dot(lhs_v[...], weight_v[slot], 1, 1)
        part[j] = p.astype(BF16)
        near_copy(j).start()

        @pl.when(j >= 1)
        def _():
            join(j - 1)

        return carry

    lax.fori_loop(0, steps, step, 0)
    join(steps - 1)

    def last(j, carry):
        total = mine[0, j].astype(F32)
        for k in range(1, chips):
            far_copy(k, j).wait()
            total = total + far[k, j].astype(F32)
        out[:, pl.ds(pl.multiple_of(j * cols, cols), cols)] = total.astype(BF16)
        return carry

    lax.fori_loop(0, steps, last, 0)
    finish(jobs)


def main_call(groups, n, lhs_q, lhs_v, query_matrix, value_matrix, activations, own_query, own_down, own_value):
    tokens, width = lhs_q.shape
    rows = activations.shape[0]
    cols = 512
    steps = query_matrix.shape[0] // cols
    chips = n // 2
    half = tokens // 2
    s = jax.ShapeDtypeStruct
    return pl.pallas_call(
        functools.partial(main_kernel, groups, n),
        out_shape=[
            s((rows, steps * cols), BF16),
            s((n, rows, width), BF16),
            s((groups,) + own_query.shape, BF16),
            s((groups,) + own_down.shape, BF16),
            s((groups,) + own_value.shape, BF16),
        ],
        in_specs=[VMEM, VMEM] + [ANY] * 6,
        out_specs=[VMEM, ANY, ANY, ANY, ANY],
        scratch_shapes=[
            pltpu.VMEM((2, cols, width), BF16),
            pltpu.VMEM((2, cols, lhs_v.shape[1]), BF16),
            pltpu.VMEM((steps, tokens, cols), BF16),
            pltpu.VMEM((steps, half, cols), BF16),
            pltpu.VMEM((chips, steps, rows, cols), BF16),
            pltpu.VMEM((chips, steps, rows, cols), BF16),
            DMA((2,)),
            DMA((2,)),
            DMA((steps,)),
            DMA((steps,)),
            DMA((chips, steps)),
            DMA((chips, steps)),
            DMA((n,)),
            DMA((n,)),
            DMA((groups,)),
            DMA((groups,)),
            DMA((groups,)),
            DMA((groups,)),
            DMA((groups,)),
            DMA((groups,)),
        ],
        compiler_params=pltpu.CompilerParams(
            collective_id=0, has_side_effects=True, vmem_limit_bytes=48 * 1024 * 1024
        ),
        name="frozen_and_gathers",
    )(lhs_q, lhs_v, query_matrix, value_matrix, activations, own_query, own_down, own_value)


def body(
    activations,
    query_cotangent,
    value_cotangent,
    query_matrix,
    value_matrix,
    block_tenant,
    owner_slot,
    slot_step,
    down_state,
    query_state,
    value_state,
    serve_tenant,
):
    G = lax.axis_size("dp")
    T = lax.axis_size("tensor")
    sizes = {"dp": G, "tensor": T}
    g = lax.axis_index("dp")
    t = lax.axis_index("tensor")
    chips = T // 2
    core, chip = t % 2, t // 2
    tokens, width = query_cotangent.shape
    value_here = value_cotangent.shape[1]
    rows = activations.shape[0]
    owned, rank = query_state.shape[0], query_state.shape[2]
    slots = owned * G
    block_len = tokens // block_tenant.shape[0]
    served_here = serve_tenant.shape[0] // G

    own_query = query_state[:, 0].astype(BF16).reshape(owned * rank, width)
    own_down = down_state[:, 0].astype(BF16).reshape(owned * 2 * rank, width)
    own_value = value_state[:, 0].astype(BF16).reshape(owned * rank, value_here)

    def ordered(a):
        cut = [
            lax.dynamic_slice_in_dim(a, (2 * ((chip + k) % chips) + c) * rows, rows, 0)
            for c in (1 - core, core)
            for k in range(chips)
        ]
        return jnp.concatenate(cut, axis=0)

    frozen, feats, all_query, all_down, all_value = main_call(
        G,
        T,
        ordered(query_cotangent),
        ordered(value_cotangent),
        query_matrix,
        value_matrix,
        activations,
        own_query,
        own_down,
        own_value,
    )
    feats = feats.reshape(tokens, width)
    work_query = all_query.reshape(slots * rank, width)
    work_down = all_down.reshape(slots * 2 * rank, width)
    work_value = all_value.reshape(slots * rank, value_here)

    position = jnp.repeat(owner_slot[block_tenant], block_len)
    mask = jnp.arange(slots, dtype=jnp.int32)[:, None, None] == position[None, None, :]

    def pick(product):
        p = product.reshape(slots, -1, tokens)
        return jnp.sum(jnp.where(mask, p, 0.0), axis=0)

    def spread(low):
        return jnp.where(mask, low[None], jnp.zeros((), BF16)).reshape(-1, tokens)

    part = jnp.concatenate(
        [
            pick(dot(work_query, query_cotangent, 1, 1)),
            pick(dot(work_value, value_cotangent, 1, 1)),
            pick(dot(work_down, feats, 1, 1)),
        ],
        axis=0,
    ).astype(BF16)
    low = add_everywhere(part, T)
    low_u, low_h = low[: 2 * rank], low[2 * rank :]
    low_u_at = spread(low_u)

    down_part = (ADAPTER_SCALE * dot(low_u_at, feats, 1, 0)).astype(BF16)
    query_part = (ADAPTER_SCALE * dot(spread(low_h[:rank]), query_cotangent, 1, 0)).astype(BF16)
    value_part = (ADAPTER_SCALE * dot(spread(low_h[rank:]), value_cotangent, 1, 0)).astype(BF16)
    lora = (ADAPTER_SCALE * dot(low_u_at, work_down, 0, 0)).astype(BF16)

    down_grad, query_grad, value_grad, lora_came = line_sums(
        [
            down_part.reshape(G, owned * 2 * rank, width),
            query_part.reshape(G, owned * rank, width),
            value_part.reshape(G, owned * rank, value_here),
        ],
        lora.reshape(T, rows, width),
        sizes,
        owned * rank,
    )

    serve_rows = owner_slot[serve_tenant].reshape(G, served_here)
    row = jnp.sum(jnp.where(serve_rows // owned == g, serve_rows % owned, 0), axis=1)
    counts = slot_step.astype(F32)
    fix = jnp.stack(
        [1.0 - jnp.exp(counts * math.log(BETA_ONE)), 1.0 - jnp.exp(counts * math.log(BETA_TWO))]
    )
    d_master, d_moments, d_wanted = adam(
        down_state.reshape(owned, 3, 2 * rank, width),
        down_grad.reshape(owned, 2 * rank, width),
        fix,
        row,
        True,
    )
    new_query, q_wanted = adam(
        query_state, query_grad.reshape(owned, rank, width), fix, row, False
    )
    new_value, v_wanted = adam(
        value_state, value_grad.reshape(owned, rank, value_here), fix, row, False
    )
    down_new, query_new, value_new = swap(
        [d_wanted, q_wanted, v_wanted], ("dp",) * 3, sizes, 3
    )
    owner = lax.dynamic_index_in_dim(serve_rows, g, 0, False) // owned

    served_down, served_query, served_value = served(owner, [down_new, query_new, value_new])

    input_cotangent = (frozen.astype(F32) + lora_came.astype(F32)).astype(BF16)

    return (
        input_cotangent,
        d_moments.reshape(owned, 2, 2, rank, width),
        d_master.reshape(owned, 2, rank, width),
        new_query,
        new_value,
        served_down.reshape(served_here, 2, rank, width),
        served_query,
        served_value,
    )


def solution(mesh):
    in_specs = (
        P(("parts", "dp", "tensor"), None),
        P(("parts", "dp"), "tensor"),
        P(("parts", "dp"), "tensor"),
        P(None, "tensor"),
        P(None, "tensor"),
        P(("parts", "dp")),
        P("parts"),
        P(("parts", "dp")),
        P(("parts", "dp"), None, None, None, "tensor"),
        P(("parts", "dp"), None, None, "tensor"),
        P(("parts", "dp"), None, None, "tensor"),
        P("parts"),
    )
    out_specs = (
        P(("parts", "dp", "tensor"), None),
        P(("parts", "dp"), None, None, None, "tensor"),
        P(("parts", "dp"), None, None, "tensor"),
        P(("parts", "dp"), None, None, "tensor"),
        P(("parts", "dp"), None, None, "tensor"),
        P(("parts", "dp"), None, None, "tensor"),
        P(("parts", "dp"), None, "tensor"),
        P(("parts", "dp"), None, "tensor"),
    )
    return jax.shard_map(body, mesh=mesh, in_specs=in_specs, out_specs=out_specs, check_vma=False)
```
